32 devices in a mesh: pp: 4 (over y, x), cp: 4 (over z), dp: 2 (over core).
Axes of the slice: x: 2, y: 2, z: 4, core: 2. Of those that a mesh axis runs over, the one named last changes fastest.
Arguments:
- queries: bfloat16 [4, 512, 1024], P('pp', 'cp', 'dp'), may hold values from -8 to 8
- keys: bfloat16 [4, 512, 128], P('pp', 'cp'), may hold values from -8 to 8
- values: bfloat16 [4, 512, 128], P('pp', 'cp'), may hold values from -6 to 6
- grad_out: bfloat16 [4, 512, 1024], P('pp', 'cp', 'dp'), may hold values from -6 to 6
- span_order: int32 [8], replicated, may hold values from 0 to 7, each once
Outputs:
- attn_out: bfloat16 [4, 512, 1024], P('pp', 'cp', 'dp')
- grad_queries: bfloat16 [4, 512, 1024], P('pp', 'cp', 'dp')
- grad_keys: bfloat16 [4, 512, 128], P('pp', 'cp')
- grad_values: bfloat16 [4, 512, 128], P('pp', 'cp')
The draws below stay inside these ranges and needn't reach their ends.
Inputs may be any that keep to these rules, and one draw needn't show every extreme that they name: Every block number appears once; the rows of index c of cp hold blocks span_order[2c] and span_order[2c + 1].
All inputs are finite; a program needn't handle non-finite values.
Results may differ from the reference program's by a relative error of at most 0.038.
Values may be sent and summed in bfloat16 or wider, within the bound.
A program may use at most 64 MiB of HBM per device.

```python
import math
import jax
import jax.numpy as jnp
from jax import lax

DH = 128
GROUP_HEADS = 8
TOK_DEV = 128
SECTIONS = 4
SEQ = 512
SPANS = 8
QW = 1024


def draw_queries(key, part):
    base = jnp.clip(jax.random.normal(jax.random.fold_in(key, 1), (SECTIONS, SEQ, QW), jnp.float32), -6.0, 6.0)
    return base.astype(jnp.bfloat16)


def draw_keys(key, part):
    base = jnp.clip(jax.random.normal(jax.random.fold_in(key, 11), (SECTIONS, SEQ, DH), jnp.float32), -6.0, 6.0)
    return base.astype(jnp.bfloat16)


def block_scale(stream_key, shape, pieces, smallest, largest):
    level = 1.0
    for position, shards_of in pieces:
        steps = jax.random.uniform(jax.random.fold_in(jax.random.fold_in(stream_key, 6), position), (shards_of,), jnp.float32, smallest / len(pieces), largest / len(pieces))
        level = level * jnp.repeat(jnp.exp(steps), shape[position] // shards_of).reshape((-1,) + (1,) * (len(shape) - 1 - position))
    return level


def normal_values(stream_key, extent, spread, most, shards=(), held_as=jnp.bfloat16):
    result = spread * jax.random.normal(stream_key, extent, jnp.float32)
    if shards:
        result = result * block_scale(stream_key, extent, shards, -0.22, 0.18)
    return jnp.clip(result, -most, most).astype(held_as)


def setup_inputs(seed: int = 0) -> dict:
    key_list = jax.random.split(jax.random.key(seed), 6)
    queries = draw_queries(jax.random.fold_in(key_list[5], 71), 0)
    keys = draw_keys(jax.random.fold_in(key_list[5], 71), 0)
    values = normal_values(key_list[2], (SECTIONS, SEQ, DH), 1.0, 6.0, ((0, 4), (1, 4)))
    grad_out = normal_values(key_list[3], (SECTIONS, SEQ, QW), 1.0, 6.0, ((0, 4), (1, 4), (2, 2)))
    span_order = jax.random.permutation(key_list[4], SPANS).astype(jnp.int32)
    return {"queries": queries, "keys": keys, "values": values, "grad_out": grad_out, "span_order": span_order}


def reference(queries, keys, values, grad_out, span_order):
    half_len = TOK_DEV // 2
    offsets = jnp.arange(half_len, dtype=jnp.int32)
    positions = (span_order[:, None].astype(jnp.int32) * half_len + offsets[None, :]).reshape(SEQ)
    causal = positions[None, :] <= positions[:, None]
    score_scale = 1.0 / math.sqrt(DH)
    incoming = jnp.roll(grad_out, -1, axis=0)

    def one_head(query_h, key_rows, value_rows, grad_h):
        scores = jnp.dot(query_h, key_rows.T, preferred_element_type=jnp.float32) * score_scale
        scores = jnp.where(causal, scores, -1e+30)
        row_peak = lax.optimization_barrier(jnp.max(scores, axis=1))
        weights = jnp.where(causal, jnp.exp(scores - row_peak[:, None]), 0.0)
        row_total = lax.optimization_barrier(jnp.sum(weights, axis=1))
        output = (jnp.dot(weights.astype(jnp.bfloat16), value_rows, preferred_element_type=jnp.float32) / row_total[:, None]).astype(jnp.bfloat16)
        log_total = row_peak + jnp.log(row_total)
        attn_prob = jnp.where(causal, jnp.exp(scores - log_total[:, None]), 0.0)
        row_dots = lax.optimization_barrier(jnp.sum(grad_h.astype(jnp.float32) * output.astype(jnp.float32), axis=1))
        grad_prob = jnp.dot(grad_h, value_rows.T, preferred_element_type=jnp.float32)
        dscore = (attn_prob * (grad_prob - row_dots[:, None])).astype(jnp.bfloat16)
        grad_query = (jnp.dot(dscore, key_rows, preferred_element_type=jnp.float32) * score_scale).astype(jnp.bfloat16)
        grad_key = jnp.dot(dscore.T, query_h, preferred_element_type=jnp.float32) * score_scale
        grad_value = jnp.dot(attn_prob.astype(jnp.bfloat16).T, grad_h, preferred_element_type=jnp.float32)
        return (output, grad_query, grad_key, grad_value)

    def one_section(section_args):
        query_rows, key_rows, value_rows, grad_rows = section_args
        query_heads = query_rows.reshape(SEQ, GROUP_HEADS, DH).transpose(1, 0, 2)
        grad_heads = grad_rows.reshape(SEQ, GROUP_HEADS, DH).transpose(1, 0, 2)

        def head_step(head_args):
            return one_head(head_args[0], key_rows, value_rows, head_args[1])
        output, grad_query, grad_key, grad_value = lax.map(head_step, (query_heads, grad_heads))
        output = output.transpose(1, 0, 2).reshape(SEQ, QW)
        grad_query = grad_query.transpose(1, 0, 2).reshape(SEQ, QW)
        grad_key = lax.optimization_barrier(jnp.sum(grad_key, axis=0)).astype(jnp.bfloat16)
        grad_value = lax.optimization_barrier(jnp.sum(grad_value, axis=0)).astype(jnp.bfloat16)
        return (output, grad_query, grad_key, grad_value)
    attn_out, grad_queries, grad_keys, grad_values = lax.map(one_section, (queries, keys, values, incoming))
    return (attn_out, grad_queries, grad_keys, grad_values)
```

```python
import functools
import math

import jax
import jax.numpy as jnp
from jax import lax
from jax.experimental import pallas as pl
from jax.experimental.pallas import tpu as pltpu
from jax.sharding import PartitionSpec as P

MESH = pl.DeviceIdType.MESH
NEG = -1e30


def each(count, fn):
    if count <= 8:
        for i in range(count):
            fn(i)
    else:

        def step(i, carry):
            fn(i)
            return carry

        lax.fori_loop(0, count, step, 0)


def kernel(
    n_pp, n, n_dp, heads, span_ref, q_ref, k_ref, v_ref, g_ref,
    o_ref, dq_ref, dk_ref, dv_ref,
    kv, qg, wts, dprob, stat, pair, xsend, xrecv, rsend, rrecv, own, fin, ovm, dqvm,
    q_sem, kv_sem, out_sem, g_send, g_recv, s_send, s_recv, f_send, f_recv,
    x_send, x_recv, r_send, r_recv, e_send, e_recv,
):
    tok, dh = kv.shape[2], kv.shape[3]
    half = tok // 2
    width = heads * dh if False else heads * tok
    scale = 1.0 / math.sqrt(dh)
    f32, bf16 = jnp.float32, jnp.bfloat16
    s = lax.axis_index("pp")
    c = lax.axis_index("cp")
    d = lax.axis_index("dp")
    other = 1 - d
    before = lax.rem(s + n_pp - 1, n_pp)
    after = lax.rem(s + 1, n_pp)

    def peer(i):
        return lax.rem(c + i, n)

    barrier = pltpu.get_barrier_semaphore()
    pl.semaphore_signal(barrier, inc=1, device_id={"pp": before}, device_id_type=MESH)
    pl.semaphore_signal(barrier, inc=1, device_id={"pp": after}, device_id_type=MESH)
    pl.semaphore_signal(barrier, inc=1, device_id={"dp": other}, device_id_type=MESH)
    each(
        n - 1,
        lambda i: pl.semaphore_signal(
            barrier, inc=1, device_id={"cp": peer(i + 1)}, device_id_type=MESH
        ),
    )

    load_k = pltpu.make_async_copy(k_ref.at[0], kv.at[0, c], kv_sem.at[0])
    load_v = pltpu.make_async_copy(v_ref.at[0], kv.at[1, c], kv_sem.at[1])
    load_k.start()
    load_v.start()
    load_q = [
        pltpu.make_async_copy(
            q_ref.at[0, :, pl.ds(h * dh, dh)], qg.at[0, pl.ds(h * tok, tok), :], q_sem.at[h]
        )
        for h in range(heads)
    ]
    for copy in load_q:
        copy.start()
    load_k.wait()
    load_v.wait()

    pl.semaphore_wait(barrier, n + 2)

    def spread(i):
        return pltpu.make_async_remote_copy(
            src_ref=kv.at[d, c], dst_ref=kv.at[d, c],
            send_sem=s_send.at[i], recv_sem=s_recv.at[c],
            device_id={"cp": peer(i)}, device_id_type=MESH,
        )

    def arrive(i):
        j = peer(i)
        return pltpu.make_async_remote_copy(
            src_ref=kv.at[d, j], dst_ref=kv.at[d, j],
            send_sem=s_send.at[i], recv_sem=s_recv.at[j],
            device_id={"cp": j}, device_id_type=MESH,
        )

    def forward(i):
        j = peer(i)
        return pltpu.make_async_remote_copy(
            src_ref=kv.at[d, j], dst_ref=kv.at[d, j],
            send_sem=f_send.at[i], recv_sem=f_recv.at[j],
            device_id={"dp": other}, device_id_type=MESH,
        )

    def forwarded(i):
        j = peer(i)
        return pltpu.make_async_remote_copy(
            src_ref=kv.at[other, j], dst_ref=kv.at[other, j],
            send_sem=f_send.at[i], recv_sem=f_recv.at[j],
            device_id={"dp": other}, device_id_type=MESH,
        )

    each(n - 1, lambda i: spread(i + 1).start())
    shift = [
        pltpu.make_async_remote_copy(
            src_ref=g_ref.at[0, :, pl.ds(h * dh, dh)],
            dst_ref=qg.at[1, pl.ds(h * tok, tok), :],
            send_sem=g_send.at[h], recv_sem=g_recv.at[h],
            device_id={"pp": before}, device_id_type=MESH,
        )
        for h in range(heads)
    ]
    for copy in shift:
        copy.start()

    row = lax.broadcasted_iota(jnp.int32, (tok, tok), 0)
    col = lax.broadcasted_iota(jnp.int32, (tok, tok), 1)
    within_row = lax.rem(row, half)
    query_pos = jnp.where(col < half, span_ref[2 * c], span_ref[2 * c + 1]) * half + lax.rem(col, half)
    nt = (((1,), (1,)), ((), ()))

    def block(j):
        return pl.ds(pl.multiple_of(j * tok, tok), tok)

    def scores_of(j):
        key_pos = jnp.where(row < half, span_ref[2 * j], span_ref[2 * j + 1]) * half + within_row
        visible = key_pos <= query_pos
        raw = lax.dot_general(kv[0, j], qg[0], nt, preferred_element_type=f32) * scale
        for h in range(heads):
            cols = slice(h * tok, (h + 1) * tok)
            part = jnp.where(visible, raw[:, cols], NEG)
            peak = jnp.max(part, axis=0, keepdims=True)
            weight = jnp.where(visible, jnp.exp(part - peak), 0.0)
            wts[j, :, cols] = weight
            stat[0, j, :, cols] = peak
            stat[1, j, :, cols] = jnp.sum(weight, axis=0, keepdims=True)

    def grads_of(j):
        grad = lax.dot_general(kv[1, j], qg[1], nt, preferred_element_type=f32)
        dprob[j] = grad
        stat[2, j] = jnp.sum(grad * wts[j], axis=0, keepdims=True)

    for copy in load_q:
        copy.wait()
    scores_of(c)

    def take(i):
        arrive(i).wait_recv()
        forward(i).start()

    each(n - 1, lambda i: take(i + 1))

    def use(i):
        forwarded(i).wait_recv()
        scores_of(peer(i))

    each(n - 1, lambda i: use(i + 1))
    for copy in shift:
        copy.wait_recv()
    each(n, lambda i: grads_of(peer(i)))

    peaks = stat[0]
    peak = jnp.max(peaks, axis=0, keepdims=True)
    factor = jnp.exp(peaks - peak)
    total = jnp.sum(factor * stat[1], axis=0, keepdims=True)
    factor = factor / total
    dots = jnp.sum(factor * stat[2], axis=0)
    stat[0] = factor

    share_scale = jnp.where(d == 0, scale, 1.0).astype(f32)
    other_scale = jnp.where(d == 0, 1.0, scale).astype(f32)

    def swap(i):
        j = peer(i)
        return pltpu.make_async_remote_copy(
            src_ref=xsend.at[j], dst_ref=xrecv.at[j],
            send_sem=x_send.at[j], recv_sem=x_recv.at[j],
            device_id={"dp": other}, device_id_type=MESH,
        )

    def deliver(i):
        return pltpu.make_async_remote_copy(
            src_ref=rsend.at[i], dst_ref=rrecv.at[c],
            send_sem=r_send.at[i], recv_sem=r_recv.at[c],
            device_id={"cp": peer(i)}, device_id_type=MESH,
        )

    def delivered(i):
        j = peer(i)
        return pltpu.make_async_remote_copy(
            src_ref=rsend.at[i], dst_ref=rrecv.at[j],
            send_sem=r_send.at[i], recv_sem=r_recv.at[j],
            device_id={"cp": j}, device_id_type=MESH,
        )

    def give(i):
        j = peer(i)
        prob = wts[j] * stat[0, j]
        pair[1, block(j), :] = prob.astype(bf16)
        pair[0, block(j), :] = (prob * (dprob[j] - dots)).astype(bf16)
        part = jnp.dot(pair[other, block(j), :], qg[other], preferred_element_type=f32)
        xsend[j] = (part * other_scale).astype(bf16)
        swap(i).start()

    each(n - 1, lambda i: give(i + 1))
    give(0)

    def keep(i):
        j = peer(i)
        part = jnp.dot(pair[d, block(j), :], qg[d], preferred_element_type=f32) * share_scale
        swap(i).wait_recv()
        return part + xrecv[j].astype(f32)

    def send(i):
        rsend[i] = keep(i).astype(bf16)
        deliver(i).start()

    each(n - 1, lambda i: send(i + 1))
    own[...] = keep(0)

    tn = (((0,), (0,)), ((), ()))
    keys_all = kv[0].reshape(n * tok, dh)
    values_all = kv[1].reshape(n * tok, dh)
    out_t = lax.dot_general(values_all, pair[1], tn, preferred_element_type=f32)
    for h in range(heads):
        ovm[:, h * dh:(h + 1) * dh] = out_t[:, h * tok:(h + 1) * tok].T.astype(bf16)
    put_o = pltpu.make_async_copy(ovm, o_ref.at[0], out_sem.at[0])
    put_o.start()
    dq_t = lax.dot_general(keys_all, pair[0], tn, preferred_element_type=f32) * scale
    for h in range(heads):
        dqvm[:, h * dh:(h + 1) * dh] = dq_t[:, h * tok:(h + 1) * tok].T.astype(bf16)
    put_q = pltpu.make_async_copy(dqvm, dq_ref.at[0], out_sem.at[1])
    put_q.start()

    def gather(i):
        delivered(i).wait_recv()
        own[...] += rrecv[peer(i)].astype(f32)

    each(n - 1, lambda i: gather(i + 1))
    fin[d] = own[...].astype(bf16)

    def final(share):
        return pltpu.make_async_remote_copy(
            src_ref=fin.at[share], dst_ref=fin.at[share],
            send_sem=e_send.at[0], recv_sem=e_recv.at[0],
            device_id={"dp": other}, device_id_type=MESH,
        )

    final(d).start()

    for copy in shift:
        copy.wait_send()

    def settle(i):
        spread(i).wait_send()
        forward(i).wait_send()
        deliver(i).wait_send()

    each(n - 1, lambda i: settle(i + 1))
    each(n, lambda i: swap(i).wait_send())
    final(other).wait_recv()
    put_k = pltpu.make_async_copy(fin.at[0], dk_ref.at[0], out_sem.at[2])
    put_v = pltpu.make_async_copy(fin.at[1], dv_ref.at[0], out_sem.at[3])
    put_k.start()
    put_v.start()
    final(d).wait_send()
    put_o.wait()
    put_q.wait()
    put_k.wait()
    put_v.wait()


def body(n_pp, n, n_dp, queries, keys, values, grad_out, span_order):
    tok, dh = keys.shape[1], keys.shape[2]
    heads = queries.shape[2] // dh
    width = heads * tok
    f32, bf16 = jnp.float32, jnp.bfloat16
    scratch = [
        ((2, n, tok, dh), bf16),
        ((2, width, dh), bf16),
        ((n, tok, width), f32),
        ((n, tok, width), f32),
        ((3, n, 1, width), f32),
        ((2, n * tok, width), bf16),
        ((n, tok, dh), bf16),
        ((n, tok, dh), bf16),
        ((n, tok, dh), bf16),
        ((n, tok, dh), bf16),
        ((tok, dh), f32),
        ((2, tok, dh), bf16),
        ((tok, heads * dh), bf16),
        ((tok, heads * dh), bf16),
    ]
    held = sum(math.prod(shape) * jnp.dtype(kind).itemsize for shape, kind in scratch)
    dma = pltpu.SemaphoreType.DMA
    sems = [heads, 2, 4, heads, heads, n, n, n, n, n, n, n, n, 1, 1]
    pairs = heads * tok * n * tok
    return pl.pallas_call(
        functools.partial(kernel, n_pp, n, n_dp, heads),
        out_shape=(
            jax.ShapeDtypeStruct(queries.shape, bf16),
            jax.ShapeDtypeStruct(queries.shape, bf16),
            jax.ShapeDtypeStruct(keys.shape, bf16),
            jax.ShapeDtypeStruct(values.shape, bf16),
        ),
        in_specs=[pl.BlockSpec(memory_space=pltpu.SMEM)]
        + [pl.BlockSpec(memory_space=pl.ANY)] * 4,
        out_specs=[pl.BlockSpec(memory_space=pl.ANY)] * 4,
        scratch_shapes=[pltpu.VMEM(shape, kind) for shape, kind in scratch]
        + [dma((count,)) for count in sems],
        compiler_params=pltpu.CompilerParams(
            collective_id=0,
            has_side_effects=True,
            vmem_limit_bytes=int(held * 1.25) + (8 << 20),
        ),
        cost_estimate=pl.CostEstimate(
            flops=12 * pairs * dh, bytes_accessed=8 * tok * heads * dh, transcendentals=pairs
        ),
        name="attention",
    )(span_order, queries, keys, values, grad_out)


def solution(mesh):
    in_specs = (
        P("pp", "cp", "dp"),
        P("pp", "cp", None),
        P("pp", "cp", None),
        P("pp", "cp", "dp"),
        P(),
    )
    out_specs = (P("pp", "cp", "dp"), P("pp", "cp", "dp"), P("pp", "cp", None), P("pp", "cp", None))
    sizes = [mesh.shape[axis] for axis in ("pp", "cp", "dp")]
    return jax.shard_map(
        functools.partial(body, *sizes),
        mesh=mesh, in_specs=in_specs, out_specs=out_specs, check_vma=False,
    )
```

```python
import functools
import math

import jax
import jax.numpy as jnp
from jax import lax
from jax.experimental import pallas as pl
from jax.experimental.pallas import tpu as pltpu
from jax.sharding import PartitionSpec as P

MESH = pl.DeviceIdType.MESH
NEG = -1e30


def each(count, fn):
    if count <= 8:
        for i in range(count):
            fn(i)
    else:

        def step(i, carry):
            fn(i)
            return carry

        lax.fori_loop(0, count, step, 0)


def kernel(
    n_pp, n, n_dp, heads, span_ref, q_ref, k_ref, v_ref, g_ref,
    o_ref, dq_ref, dk_ref, dv_ref,
    kv, qg, wts, dprob, stat, pair, xsend, xrecv, rsend, rrecv, own, fin,
    q_sem, kv_sem, g_send, g_recv, s_send, s_recv, f_send, f_recv,
    x_send, x_recv, r_send, r_recv, e_send, e_recv,
):
    tok, dh = kv.shape[2], kv.shape[3]
    half = tok // 2
    scale = 1.0 / math.sqrt(dh)
    f32, bf16 = jnp.float32, jnp.bfloat16
    s = lax.axis_index("pp")
    c = lax.axis_index("cp")
    d = lax.axis_index("dp")
    other = 1 - d
    before = lax.rem(s + n_pp - 1, n_pp)
    after = lax.rem(s + 1, n_pp)

    def peer(i):
        return lax.rem(c + i, n)

    barrier = pltpu.get_barrier_semaphore()
    pl.semaphore_signal(barrier, inc=1, device_id={"pp": before}, device_id_type=MESH)
    pl.semaphore_signal(barrier, inc=1, device_id={"pp": after}, device_id_type=MESH)
    pl.semaphore_signal(barrier, inc=1, device_id={"dp": other}, device_id_type=MESH)
    each(
        n - 1,
        lambda i: pl.semaphore_signal(
            barrier, inc=1, device_id={"cp": peer(i + 1)}, device_id_type=MESH
        ),
    )

    load_k = pltpu.make_async_copy(k_ref.at[0], kv.at[0, c], kv_sem.at[0])
    load_v = pltpu.make_async_copy(v_ref.at[0], kv.at[1, c], kv_sem.at[1])
    load_k.start()
    load_v.start()
    load_q = [
        pltpu.make_async_copy(
            q_ref.at[0, :, pl.ds(h * dh, dh)], qg.at[0, pl.ds(h * tok, tok), :], q_sem.at[h]
        )
        for h in range(heads)
    ]
    for copy in load_q:
        copy.start()
    load_k.wait()
    load_v.wait()

    pl.semaphore_wait(barrier, n + 2)

    def spread(i):
        return pltpu.make_async_remote_copy(
            src_ref=kv.at[d, c], dst_ref=kv.at[d, c],
            send_sem=s_send.at[i], recv_sem=s_recv.at[c],
            device_id={"cp": peer(i)}, device_id_type=MESH,
        )

    def arrive(i):
        j = peer(i)
        return pltpu.make_async_remote_copy(
            src_ref=kv.at[d, j], dst_ref=kv.at[d, j],
            send_sem=s_send.at[i], recv_sem=s_recv.at[j],
            device_id={"cp": j}, device_id_type=MESH,
        )

    def forward(i):
        j = peer(i)
        return pltpu.make_async_remote_copy(
            src_ref=kv.at[d, j], dst_ref=kv.at[d, j],
            send_sem=f_send.at[i], recv_sem=f_recv.at[j],
            device_id={"dp": other}, device_id_type=MESH,
        )

    def forwarded(i):
        j = peer(i)
        return pltpu.make_async_remote_copy(
            src_ref=kv.at[other, j], dst_ref=kv.at[other, j],
            send_sem=f_send.at[i], recv_sem=f_recv.at[j],
            device_id={"dp": other}, device_id_type=MESH,
        )

    each(n - 1, lambda i: spread(i + 1).start())
    shift = [
        pltpu.make_async_remote_copy(
            src_ref=g_ref.at[0, :, pl.ds(h * dh, dh)],
            dst_ref=qg.at[1, pl.ds(h * tok, tok), :],
            send_sem=g_send.at[h], recv_sem=g_recv.at[h],
            device_id={"pp": before}, device_id_type=MESH,
        )
        for h in range(heads)
    ]
    for copy in shift:
        copy.start()

    row = lax.broadcasted_iota(jnp.int32, (tok, tok), 0)
    col = lax.broadcasted_iota(jnp.int32, (tok, tok), 1)
    within_row = lax.rem(row, half)
    query_pos = jnp.where(col < half, span_ref[2 * c], span_ref[2 * c + 1]) * half + lax.rem(col, half)
    nt = (((1,), (1,)), ((), ()))

    def block(j):
        return pl.ds(pl.multiple_of(j * tok, tok), tok)

    def scores_of(j):
        key_pos = jnp.where(row < half, span_ref[2 * j], span_ref[2 * j + 1]) * half + within_row
        visible = key_pos <= query_pos
        raw = lax.dot_general(kv[0, j], qg[0], nt, preferred_element_type=f32) * scale
        for h in range(heads):
            cols = slice(h * tok, (h + 1) * tok)
            part = jnp.where(visible, raw[:, cols], NEG)
            peak = jnp.max(part, axis=0, keepdims=True)
            weight = jnp.where(visible, jnp.exp(part - peak), 0.0)
            wts[j, :, cols] = weight
            stat[0, j, :, cols] = peak
            stat[1, j, :, cols] = jnp.sum(weight, axis=0, keepdims=True)

    def grads_of(j):
        grad = lax.dot_general(kv[1, j], qg[1], nt, preferred_element_type=f32)
        dprob[j] = grad
        stat[2, j] = jnp.sum(grad * wts[j], axis=0, keepdims=True)

    for copy in load_q:
        copy.wait()
    scores_of(c)

    def take(i):
        arrive(i).wait_recv()
        forward(i).start()

    each(n - 1, lambda i: take(i + 1))

    def use(i):
        forwarded(i).wait_recv()
        scores_of(peer(i))

    each(n - 1, lambda i: use(i + 1))
    for copy in shift:
        copy.wait_recv()
    each(n, lambda i: grads_of(peer(i)))

    peaks = stat[0]
    peak = jnp.max(peaks, axis=0, keepdims=True)
    factor = jnp.exp(peaks - peak)
    total = jnp.sum(factor * stat[1], axis=0, keepdims=True)
    factor = factor / total
    dots = jnp.sum(factor * stat[2], axis=0)
    stat[0] = factor

    share_scale = jnp.where(d == 0, scale, 1.0).astype(f32)
    other_scale = jnp.where(d == 0, 1.0, scale).astype(f32)

    def swap(i):
        j = peer(i)
        return pltpu.make_async_remote_copy(
            src_ref=xsend.at[j], dst_ref=xrecv.at[j],
            send_sem=x_send.at[j], recv_sem=x_recv.at[j],
            device_id={"dp": other}, device_id_type=MESH,
        )

    def deliver(i):
        return pltpu.make_async_remote_copy(
            src_ref=rsend.at[i], dst_ref=rrecv.at[c],
            send_sem=r_send.at[i], recv_sem=r_recv.at[c],
            device_id={"cp": peer(i)}, device_id_type=MESH,
        )

    def delivered(i):
        j = peer(i)
        return pltpu.make_async_remote_copy(
            src_ref=rsend.at[i], dst_ref=rrecv.at[j],
            send_sem=r_send.at[i], recv_sem=r_recv.at[j],
            device_id={"cp": j}, device_id_type=MESH,
        )

    def give(i):
        j = peer(i)
        prob = wts[j] * stat[0, j]
        pair[1, block(j), :] = prob.astype(bf16)
        pair[0, block(j), :] = (prob * (dprob[j] - dots)).astype(bf16)
        part = jnp.dot(pair[other, block(j), :], qg[other], preferred_element_type=f32)
        xsend[j] = (part * other_scale).astype(bf16)
        swap(i).start()

    each(n - 1, lambda i: give(i + 1))
    give(0)

    def keep(i):
        j = peer(i)
        part = jnp.dot(pair[d, block(j), :], qg[d], preferred_element_type=f32) * share_scale
        swap(i).wait_recv()
        return part + xrecv[j].astype(f32)

    def send(i):
        rsend[i] = keep(i).astype(bf16)
        deliver(i).start()

    each(n - 1, lambda i: send(i + 1))
    own[...] = keep(0)

    tn = (((0,), (0,)), ((), ()))
    keys_all = kv[0].reshape(n * tok, dh)
    values_all = kv[1].reshape(n * tok, dh)
    out_t = lax.dot_general(values_all, pair[1], tn, preferred_element_type=f32)
    for h in range(heads):
        o_ref[0, :, h * dh:(h + 1) * dh] = out_t[:, h * tok:(h + 1) * tok].T.astype(bf16)
    dq_t = lax.dot_general(keys_all, pair[0], tn, preferred_element_type=f32) * scale
    for h in range(heads):
        dq_ref[0, :, h * dh:(h + 1) * dh] = dq_t[:, h * tok:(h + 1) * tok].T.astype(bf16)

    def gather(i):
        delivered(i).wait_recv()
        own[...] += rrecv[peer(i)].astype(f32)

    each(n - 1, lambda i: gather(i + 1))
    fin[d] = own[...].astype(bf16)

    def final(share):
        return pltpu.make_async_remote_copy(
            src_ref=fin.at[share], dst_ref=fin.at[share],
            send_sem=e_send.at[0], recv_sem=e_recv.at[0],
            device_id={"dp": other}, device_id_type=MESH,
        )

    final(d).start()

    for copy in shift:
        copy.wait_send()

    def settle(i):
        spread(i).wait_send()
        forward(i).wait_send()
        deliver(i).wait_send()

    each(n - 1, lambda i: settle(i + 1))
    each(n, lambda i: swap(i).wait_send())
    final(other).wait_recv()
    dk_ref[0] = fin[0]
    dv_ref[0] = fin[1]
    final(d).wait_send()


def writer(*refs):
    count = len(refs) // 2
    sem = refs[-1]
    copies = [
        pltpu.make_async_copy(refs[i], refs[count + i], sem.at[i]) for i in range(count)
    ]
    for copy in copies:
        copy.start()
    for copy in copies:
        copy.wait()


def body(n_pp, n, n_dp, queries, keys, values, grad_out, span_order):
    tok, dh = keys.shape[1], keys.shape[2]
    heads = queries.shape[2] // dh
    width = heads * tok
    f32, bf16 = jnp.float32, jnp.bfloat16
    scratch = [
        ((2, n, tok, dh), bf16),
        ((2, width, dh), bf16),
        ((n, tok, width), f32),
        ((n, tok, width), f32),
        ((3, n, 1, width), f32),
        ((2, n * tok, width), bf16),
        ((n, tok, dh), bf16),
        ((n, tok, dh), bf16),
        ((n, tok, dh), bf16),
        ((n, tok, dh), bf16),
        ((tok, dh), f32),
        ((2, tok, dh), bf16),
    ]
    held = sum(math.prod(shape) * jnp.dtype(kind).itemsize for shape, kind in scratch)
    dma = pltpu.SemaphoreType.DMA
    sems = [heads, 2, heads, heads, n, n, n, n, n, n, n, n, 1, 1]
    pairs = heads * tok * n * tok
    results = pl.pallas_call(
        functools.partial(kernel, n_pp, n, n_dp, heads),
        out_shape=(
            pltpu.VMEM(queries.shape, bf16),
            pltpu.VMEM(queries.shape, bf16),
            pltpu.VMEM(keys.shape, bf16),
            pltpu.VMEM(values.shape, bf16),
        ),
        in_specs=[pl.BlockSpec(memory_space=pltpu.SMEM)]
        + [pl.BlockSpec(memory_space=pltpu.HBM)] * 4,
        out_specs=[pl.BlockSpec(memory_space=pltpu.VMEM)] * 4,
        scratch_shapes=[pltpu.VMEM(shape, kind) for shape, kind in scratch]
        + [dma((count,)) for count in sems],
        compiler_params=pltpu.CompilerParams(
            collective_id=0,
            has_side_effects=True,
            vmem_limit_bytes=60 << 20,
        ),
        cost_estimate=pl.CostEstimate(
            flops=12 * pairs * dh, bytes_accessed=8 * tok * heads * dh, transcendentals=pairs
        ),
        name="attention",
    )(span_order, queries, keys, values, grad_out)
    return pl.pallas_call(
        writer,
        out_shape=[jax.ShapeDtypeStruct(r.shape, r.dtype) for r in results],
        in_specs=[pl.BlockSpec(memory_space=pl.ANY)] * 4,
        out_specs=[pl.BlockSpec(memory_space=pltpu.HBM)] * 4,
        scratch_shapes=[dma((4,))],
        compiler_params=pltpu.CompilerParams(vmem_limit_bytes=4 << 20),
        name="writer",
    )(*results)


def solution(mesh):
    in_specs = (
        P("pp", "cp", "dp"),
        P("pp", "cp", None),
        P("pp", "cp", None),
        P("pp", "cp", "dp"),
        P(),
    )
    out_specs = (P("pp", "cp", "dp"), P("pp", "cp", "dp"), P("pp", "cp", None), P("pp", "cp", None))
    sizes = [mesh.shape[axis] for axis in ("pp", "cp", "dp")]
    return jax.shard_map(
        functools.partial(body, *sizes),
        mesh=mesh, in_specs=in_specs, out_specs=out_specs, check_vma=False,
    )
```

```python
import functools
import math

import jax
import jax.numpy as jnp
from jax import lax
from jax.experimental import pallas as pl
from jax.experimental.pallas import tpu as pltpu
from jax.sharding import PartitionSpec as P

MESH = pl.DeviceIdType.MESH
NEG = -1e30


def each(count, fn):
    if count <= 8:
        for i in range(count):
            fn(i)
    else:

        def step(i, carry):
            fn(i)
            return carry

        lax.fori_loop(0, count, step, 0)


def kernel(
    n_pp, n, n_dp, heads, span_ref, q_ref, k_ref, v_ref, g_ref,
    o_ref, dq_ref, dk_ref, dv_ref,
    kv, qg, wts, dprob, stat, pair, xsend, xrecv, rsend, rrecv, own, fin,
    q_sem, kv_sem, g_send, g_recv, s_send, s_recv, f_send, f_recv,
    x_send, x_recv, r_send, r_recv, e_send, e_recv,
):
    tok, dh = kv.shape[2], kv.shape[3]
    half = tok // 2
    scale = 1.0 / math.sqrt(dh)
    f32, bf16 = jnp.float32, jnp.bfloat16
    s = lax.axis_index("pp")
    c = lax.axis_index("cp")
    d = lax.axis_index("dp")
    other = 1 - d
    before = lax.rem(s + n_pp - 1, n_pp)
    after = lax.rem(s + 1, n_pp)

    def rising(i):
        return i - 1 + (i - 1 - c + n) // n

    def falling(i):
        return rising(n - i)

    def nearing(i):
        wrapped = (c + i) // n
        return (1 - wrapped) * (c + i) + wrapped * (n - 1 - i)

    barrier = pltpu.get_barrier_semaphore()
    each(
        n - 1,
        lambda i: pl.semaphore_signal(
            barrier, inc=1, device_id={"cp": rising(i + 1)}, device_id_type=MESH
        ),
    )
    pl.semaphore_signal(barrier, inc=1, device_id={"pp": before}, device_id_type=MESH)
    pl.semaphore_signal(barrier, inc=1, device_id={"pp": after}, device_id_type=MESH)
    pl.semaphore_signal(barrier, inc=1, device_id={"dp": other}, device_id_type=MESH)

    load_k = pltpu.make_async_copy(k_ref.at[0], kv.at[0, c], kv_sem.at[0])
    load_v = pltpu.make_async_copy(v_ref.at[0], kv.at[1, c], kv_sem.at[1])
    load_k.start()
    load_v.start()
    load_q = [
        pltpu.make_async_copy(
            q_ref.at[0, :, pl.ds(h * dh, dh)], qg.at[0, pl.ds(h * tok, tok), :], q_sem.at[h]
        )
        for h in range(heads)
    ]
    for copy in load_q:
        copy.start()
    load_k.wait()
    load_v.wait()

    pl.semaphore_wait(barrier, n + 2)

    def spread(j):
        return pltpu.make_async_remote_copy(
            src_ref=kv.at[d, c], dst_ref=kv.at[d, c],
            send_sem=s_send.at[j], recv_sem=s_recv.at[c],
            device_id={"cp": j}, device_id_type=MESH,
        )

    def arrive(j):
        return pltpu.make_async_remote_copy(
            src_ref=kv.at[d, j], dst_ref=kv.at[d, j],
            send_sem=s_send.at[j], recv_sem=s_recv.at[j],
            device_id={"cp": j}, device_id_type=MESH,
        )

    def forward(j):
        return pltpu.make_async_remote_copy(
            src_ref=kv.at[d, j], dst_ref=kv.at[d, j],
            send_sem=f_send.at[j], recv_sem=f_recv.at[j],
            device_id={"dp": other}, device_id_type=MESH,
        )

    def forwarded(j):
        return pltpu.make_async_remote_copy(
            src_ref=kv.at[other, j], dst_ref=kv.at[other, j],
            send_sem=f_send.at[j], recv_sem=f_recv.at[j],
            device_id={"dp": other}, device_id_type=MESH,
        )

    each(n - 1, lambda i: spread(falling(i + 1)).start())
    shift = [
        pltpu.make_async_remote_copy(
            src_ref=g_ref.at[0, :, pl.ds(h * dh, dh)],
            dst_ref=qg.at[1, pl.ds(h * tok, tok), :],
            send_sem=g_send.at[h], recv_sem=g_recv.at[h],
            device_id={"pp": before}, device_id_type=MESH,
        )
        for h in range(heads)
    ]
    for copy in shift:
        copy.start()

    row = lax.broadcasted_iota(jnp.int32, (tok, tok), 0)
    col = lax.broadcasted_iota(jnp.int32, (tok, tok), 1)
    within_row = lax.rem(row, half)
    query_pos = jnp.where(col < half, span_ref[2 * c], span_ref[2 * c + 1]) * half + lax.rem(col, half)
    nt = (((1,), (1,)), ((), ()))

    def block(j):
        return pl.ds(pl.multiple_of(j * tok, tok), tok)

    def scores_of(j):
        key_pos = jnp.where(row < half, span_ref[2 * j], span_ref[2 * j + 1]) * half + within_row
        visible = key_pos <= query_pos
        raw = lax.dot_general(kv[0, j], qg[0], nt, preferred_element_type=f32) * scale
        for h in range(heads):
            cols = slice(h * tok, (h + 1) * tok)
            part = jnp.where(visible, raw[:, cols], NEG)
            peak = jnp.max(part, axis=0, keepdims=True)
            weight = jnp.where(visible, jnp.exp(part - peak), 0.0)
            wts[j, :, cols] = weight
            stat[0, j, :, cols] = peak
            stat[1, j, :, cols] = jnp.sum(weight, axis=0, keepdims=True)

    def grads_of(j):
        grad = lax.dot_general(kv[1, j], qg[1], nt, preferred_element_type=f32)
        dprob[j] = grad
        stat[2, j] = jnp.sum(grad * wts[j], axis=0, keepdims=True)

    for copy in load_q:
        copy.wait()
    scores_of(c)

    def take(i):
        arrive(nearing(i)).wait_recv()
        forward(nearing(i)).start()

    def use(i):
        forwarded(nearing(i)).wait_recv()
        scores_of(nearing(i))

    def take_and_use(i):
        take(i + 2)
        use(i + 1)

    take(1)
    each(n - 2, take_and_use)
    for copy in shift:
        copy.wait_recv()
    grads_of(c)
    each(n - 2, lambda i: grads_of(nearing(i + 1)))
    use(n - 1)
    grads_of(nearing(n - 1))

    peaks = stat[0]
    peak = jnp.max(peaks, axis=0, keepdims=True)
    factor = jnp.exp(peaks - peak)
    total = jnp.sum(factor * stat[1], axis=0, keepdims=True)
    factor = factor / total
    dots = jnp.sum(factor * stat[2], axis=0)
    stat[0] = factor

    share_scale = jnp.where(d == 0, scale, 1.0).astype(f32)
    other_scale = jnp.where(d == 0, 1.0, scale).astype(f32)

    def swap(j):
        return pltpu.make_async_remote_copy(
            src_ref=xsend.at[j], dst_ref=xrecv.at[j],
            send_sem=x_send.at[j], recv_sem=x_recv.at[j],
            device_id={"dp": other}, device_id_type=MESH,
        )

    def deliver(j):
        return pltpu.make_async_remote_copy(
            src_ref=rsend.at[j], dst_ref=rrecv.at[c],
            send_sem=r_send.at[j], recv_sem=r_recv.at[c],
            device_id={"cp": j}, device_id_type=MESH,
        )

    def delivered(j):
        return pltpu.make_async_remote_copy(
            src_ref=rsend.at[j], dst_ref=rrecv.at[j],
            send_sem=r_send.at[j], recv_sem=r_recv.at[j],
            device_id={"cp": j}, device_id_type=MESH,
        )

    def give(j):
        prob = wts[j] * stat[0, j]
        pair[1, block(j), :] = prob.astype(bf16)
        pair[0, block(j), :] = (prob * (dprob[j] - dots)).astype(bf16)
        part = jnp.dot(pair[other, block(j), :], qg[other], preferred_element_type=f32)
        xsend[j] = (part * other_scale).astype(bf16)
        swap(j).start()

    each(n - 1, lambda i: give(rising(i + 1)))
    give(c)

    def keep(j):
        part = jnp.dot(pair[d, block(j), :], qg[d], preferred_element_type=f32) * share_scale
        swap(j).wait_recv()
        return part + xrecv[j].astype(f32)

    def send(j):
        rsend[j] = keep(j).astype(bf16)
        deliver(j).start()

    each(n - 1, lambda i: send(rising(i + 1)))
    own[...] = keep(c)

    tn = (((0,), (0,)), ((), ()))
    keys_all = kv[0].reshape(n * tok, dh)
    values_all = kv[1].reshape(n * tok, dh)
    out_t = lax.dot_general(values_all, pair[1], tn, preferred_element_type=f32)
    for h in range(heads):
        o_ref[0, :, h * dh:(h + 1) * dh] = out_t[:, h * tok:(h + 1) * tok].T.astype(bf16)
    dq_t = lax.dot_general(keys_all, pair[0], tn, preferred_element_type=f32) * scale
    for h in range(heads):
        dq_ref[0, :, h * dh:(h + 1) * dh] = dq_t[:, h * tok:(h + 1) * tok].T.astype(bf16)

    def gather(j):
        delivered(j).wait_recv()
        own[...] += rrecv[j].astype(f32)

    each(n - 1, lambda i: gather(rising(i + 1)))
    fin[d] = own[...].astype(bf16)

    def final(share):
        return pltpu.make_async_remote_copy(
            src_ref=fin.at[share], dst_ref=fin.at[share],
            send_sem=e_send.at[0], recv_sem=e_recv.at[0],
            device_id={"dp": other}, device_id_type=MESH,
        )

    final(d).start()

    for copy in shift:
        copy.wait_send()

    def settle(j):
        spread(j).wait_send()
        forward(j).wait_send()
        deliver(j).wait_send()

    each(n - 1, lambda i: settle(rising(i + 1)))
    each(n, lambda j: swap(j).wait_send())
    final(other).wait_recv()
    dk_ref[0] = fin[0]
    dv_ref[0] = fin[1]
    final(d).wait_send()


def writer(*refs):
    count = len(refs) // 2
    sem = refs[-1]
    copies = [
        pltpu.make_async_copy(refs[i], refs[count + i], sem.at[i]) for i in range(count)
    ]
    for copy in copies:
        copy.start()
    for copy in copies:
        copy.wait()


def body(n_pp, n, n_dp, queries, keys, values, grad_out, span_order):
    tok, dh = keys.shape[1], keys.shape[2]
    heads = queries.shape[2] // dh
    width = heads * tok
    f32, bf16 = jnp.float32, jnp.bfloat16
    scratch = [
        ((2, n, tok, dh), bf16),
        ((2, width, dh), bf16),
        ((n, tok, width), f32),
        ((n, tok, width), f32),
        ((3, n, 1, width), f32),
        ((2, n * tok, width), bf16),
        ((n, tok, dh), bf16),
        ((n, tok, dh), bf16),
        ((n, tok, dh), bf16),
        ((n, tok, dh), bf16),
        ((tok, dh), f32),
        ((2, tok, dh), bf16),
    ]
    held = sum(math.prod(shape) * jnp.dtype(kind).itemsize for shape, kind in scratch)
    dma = pltpu.SemaphoreType.DMA
    sems = [heads, 2, heads, heads, n, n, n, n, n, n, n, n, 1, 1]
    pairs = heads * tok * n * tok
    results = pl.pallas_call(
        functools.partial(kernel, n_pp, n, n_dp, heads),
        out_shape=(
            pltpu.VMEM(queries.shape, bf16),
            pltpu.VMEM(queries.shape, bf16),
            pltpu.VMEM(keys.shape, bf16),
            pltpu.VMEM(values.shape, bf16),
        ),
        in_specs=[pl.BlockSpec(memory_space=pltpu.SMEM)]
        + [pl.BlockSpec(memory_space=pltpu.HBM)] * 4,
        out_specs=[pl.BlockSpec(memory_space=pltpu.VMEM)] * 4,
        scratch_shapes=[pltpu.VMEM(shape, kind) for shape, kind in scratch]
        + [dma((count,)) for count in sems],
        compiler_params=pltpu.CompilerParams(
            collective_id=0,
            has_side_effects=True,
            vmem_limit_bytes=60 << 20,
        ),
        cost_estimate=pl.CostEstimate(
            flops=12 * pairs * dh, bytes_accessed=8 * tok * heads * dh, transcendentals=pairs
        ),
        name="attention",
    )(span_order, queries, keys, values, grad_out)
    return pl.pallas_call(
        writer,
        out_shape=[jax.ShapeDtypeStruct(r.shape, r.dtype) for r in results],
        in_specs=[pl.BlockSpec(memory_space=pl.ANY)] * 4,
        out_specs=[pl.BlockSpec(memory_space=pltpu.HBM)] * 4,
        scratch_shapes=[dma((4,))],
        compiler_params=pltpu.CompilerParams(vmem_limit_bytes=4 << 20),
        name="writer",
    )(*results)


def solution(mesh):
    in_specs = (
        P("pp", "cp", "dp"),
        P("pp", "cp", None),
        P("pp", "cp", None),
        P("pp", "cp", "dp"),
        P(),
    )
    out_specs = (P("pp", "cp", "dp"), P("pp", "cp", "dp"), P("pp", "cp", None), P("pp", "cp", None))
    sizes = [mesh.shape[axis] for axis in ("pp", "cp", "dp")]
    return jax.shard_map(
        functools.partial(body, *sizes),
        mesh=mesh, in_specs=in_specs, out_specs=out_specs, check_vma=False,
    )
```

```python
import functools
import math

import jax
import jax.numpy as jnp
from jax import lax
from jax.experimental import pallas as pl
from jax.experimental.pallas import tpu as pltpu
from jax.sharding import PartitionSpec as P

MESH = pl.DeviceIdType.MESH
NEG = -1e30


def each(count, fn):
    if count <= 8:
        for i in range(count):
            fn(i)
    else:

        def step(i, carry):
            fn(i)
            return carry

        lax.fori_loop(0, count, step, 0)


def kernel(
    n_pp, n, n_dp, heads, span_hbm, q_ref, k_ref, v_ref, g_ref,
    o_ref, dq_ref, dk_ref, dv_ref,
    kv, qg, wts, dprob, stat, pair, xsend, xrecv, rsend, rrecv, own, fin, span_ref,
    span_sem, q_sem, kv_sem, g_send, g_recv, s_send, s_recv, f_send, f_recv,
    x_send, x_recv, r_send, r_recv, e_send, e_recv,
):
    tok, dh = kv.shape[2], kv.shape[3]
    half = tok // 2
    scale = 1.0 / math.sqrt(dh)
    f32, bf16 = jnp.float32, jnp.bfloat16
    s = lax.axis_index("pp")
    c = lax.axis_index("cp")
    d = lax.axis_index("dp")
    other = 1 - d
    before = lax.rem(s + n_pp - 1, n_pp)
    after = lax.rem(s + 1, n_pp)

    def rising(i):
        return i - 1 + (i - 1 - c + n) // n

    def falling(i):
        return rising(n - i)

    def nearing(i):
        wrapped = (c + i) // n
        return (1 - wrapped) * (c + i) + wrapped * (n - 1 - i)

    barrier = pltpu.get_barrier_semaphore()
    each(
        n - 1,
        lambda i: pl.semaphore_signal(
            barrier, inc=1, device_id={"cp": rising(i + 1)}, device_id_type=MESH
        ),
    )
    pl.semaphore_signal(barrier, inc=1, device_id={"pp": after}, device_id_type=MESH)
    pl.semaphore_signal(barrier, inc=1, device_id={"dp": other}, device_id_type=MESH)

    load_k = pltpu.make_async_copy(k_ref.at[0], kv.at[0, c], kv_sem.at[0])
    load_v = pltpu.make_async_copy(v_ref.at[0], kv.at[1, c], kv_sem.at[1])
    load_k.start()
    load_v.start()
    load_q = [
        pltpu.make_async_copy(
            q_ref.at[0, :, pl.ds(h * dh, dh)], qg.at[0, pl.ds(h * tok, tok), :], q_sem.at[h]
        )
        for h in range(heads)
    ]
    for copy in load_q:
        copy.start()
    load_span = pltpu.make_async_copy(span_hbm, span_ref, span_sem.at[0])
    load_span.start()
    load_k.wait()
    load_v.wait()

    pl.semaphore_wait(barrier, n + 1)

    def spread(j):
        return pltpu.make_async_remote_copy(
            src_ref=kv.at[d, c], dst_ref=kv.at[d, c],
            send_sem=s_send.at[j], recv_sem=s_recv.at[c],
            device_id={"cp": j}, device_id_type=MESH,
        )

    def arrive(j):
        return pltpu.make_async_remote_copy(
            src_ref=kv.at[d, j], dst_ref=kv.at[d, j],
            send_sem=s_send.at[j], recv_sem=s_recv.at[j],
            device_id={"cp": j}, device_id_type=MESH,
        )

    def forward(j):
        return pltpu.make_async_remote_copy(
            src_ref=kv.at[d, j], dst_ref=kv.at[d, j],
            send_sem=f_send.at[j], recv_sem=f_recv.at[j],
            device_id={"dp": other}, device_id_type=MESH,
        )

    def forwarded(j):
        return pltpu.make_async_remote_copy(
            src_ref=kv.at[other, j], dst_ref=kv.at[other, j],
            send_sem=f_send.at[j], recv_sem=f_recv.at[j],
            device_id={"dp": other}, device_id_type=MESH,
        )

    each(n - 1, lambda i: spread(falling(i + 1)).start())
    shift = [
        pltpu.make_async_remote_copy(
            src_ref=g_ref.at[0, :, pl.ds(h * dh, dh)],
            dst_ref=qg.at[1, pl.ds(h * tok, tok), :],
            send_sem=g_send.at[h], recv_sem=g_recv.at[h],
            device_id={"pp": before}, device_id_type=MESH,
        )
        for h in range(heads)
    ]
    for copy in shift:
        copy.start()

    load_span.wait()
    row = lax.broadcasted_iota(jnp.int32, (tok, tok), 0)
    col = lax.broadcasted_iota(jnp.int32, (tok, tok), 1)
    within_row = lax.rem(row, half)
    query_pos = jnp.where(col < half, span_ref[2 * c], span_ref[2 * c + 1]) * half + lax.rem(col, half)
    nt = (((1,), (1,)), ((), ()))

    def block(j):
        return pl.ds(pl.multiple_of(j * tok, tok), tok)

    def scores_of(j):
        key_pos = jnp.where(row < half, span_ref[2 * j], span_ref[2 * j + 1]) * half + within_row
        visible = key_pos <= query_pos
        raw = lax.dot_general(kv[0, j], qg[0], nt, preferred_element_type=f32) * scale
        for h in range(heads):
            cols = slice(h * tok, (h + 1) * tok)
            part = jnp.where(visible, raw[:, cols], NEG)
            peak = jnp.max(part, axis=0, keepdims=True)
            weight = jnp.where(visible, jnp.exp(part - peak), 0.0)
            wts[j, :, cols] = weight
            stat[0, j, :, cols] = peak
            stat[1, j, :, cols] = jnp.sum(weight, axis=0, keepdims=True)

    def grads_of(j):
        grad = lax.dot_general(kv[1, j], qg[1], nt, preferred_element_type=f32)
        dprob[j] = grad
        stat[2, j] = jnp.sum(grad * wts[j], axis=0, keepdims=True)

    for copy in load_q:
        copy.wait()
    scores_of(c)

    def take(i):
        arrive(nearing(i)).wait_recv()
        forward(nearing(i)).start()

    def use(i):
        forwarded(nearing(i)).wait_recv()
        scores_of(nearing(i))

    def take_and_use(i):
        take(i + 2)
        use(i + 1)

    each(n - 1, lambda i: take(i + 1))
    each(n - 2, lambda i: use(i + 1))
    for copy in shift:
        copy.wait_recv()
    grads_of(c)
    each(n - 2, lambda i: grads_of(nearing(i + 1)))
    use(n - 1)
    grads_of(nearing(n - 1))

    peaks = stat[0]
    peak = jnp.max(peaks, axis=0, keepdims=True)
    factor = jnp.exp(peaks - peak)
    total = jnp.sum(factor * stat[1], axis=0, keepdims=True)
    factor = factor / total
    dots = jnp.sum(factor * stat[2], axis=0)
    stat[0] = factor

    share_scale = jnp.where(d == 0, scale, 1.0).astype(f32)
    other_scale = jnp.where(d == 0, 1.0, scale).astype(f32)

    def swap(j):
        return pltpu.make_async_remote_copy(
            src_ref=xsend.at[j], dst_ref=xrecv.at[j],
            send_sem=x_send.at[j], recv_sem=x_recv.at[j],
            device_id={"dp": other}, device_id_type=MESH,
        )

    def deliver(j):
        return pltpu.make_async_remote_copy(
            src_ref=rsend.at[j], dst_ref=rrecv.at[c],
            send_sem=r_send.at[j], recv_sem=r_recv.at[c],
            device_id={"cp": j}, device_id_type=MESH,
        )

    def delivered(j):
        return pltpu.make_async_remote_copy(
            src_ref=rsend.at[j], dst_ref=rrecv.at[j],
            send_sem=r_send.at[j], recv_sem=r_recv.at[j],
            device_id={"cp": j}, device_id_type=MESH,
        )

    def give(j):
        prob = wts[j] * stat[0, j]
        pair[1, block(j), :] = prob.astype(bf16)
        pair[0, block(j), :] = (prob * (dprob[j] - dots)).astype(bf16)
        part = jnp.dot(pair[other, block(j), :], qg[other], preferred_element_type=f32)
        xsend[j] = (part * other_scale).astype(bf16)
        swap(j).start()

    each(n - 1, lambda i: give(rising(i + 1)))
    give(c)

    def keep(j):
        part = jnp.dot(pair[d, block(j), :], qg[d], preferred_element_type=f32) * share_scale
        swap(j).wait_recv()
        return part + xrecv[j].astype(f32)

    def send(j):
        rsend[j] = keep(j).astype(bf16)
        deliver(j).start()

    each(n - 1, lambda i: send(rising(i + 1)))
    own[...] = keep(c)

    tn = (((0,), (0,)), ((), ()))
    keys_all = kv[0].reshape(n * tok, dh)
    values_all = kv[1].reshape(n * tok, dh)
    out_t = lax.dot_general(values_all, pair[1], tn, preferred_element_type=f32)
    for h in range(heads):
        o_ref[0, :, h * dh:(h + 1) * dh] = out_t[:, h * tok:(h + 1) * tok].T.astype(bf16)
    dq_t = lax.dot_general(keys_all, pair[0], tn, preferred_element_type=f32) * scale
    for h in range(heads):
        dq_ref[0, :, h * dh:(h + 1) * dh] = dq_t[:, h * tok:(h + 1) * tok].T.astype(bf16)

    def gather(j):
        delivered(j).wait_recv()
        own[...] += rrecv[j].astype(f32)

    each(n - 1, lambda i: gather(rising(i + 1)))
    fin[d] = own[...].astype(bf16)

    def final(share):
        return pltpu.make_async_remote_copy(
            src_ref=fin.at[share], dst_ref=fin.at[share],
            send_sem=e_send.at[0], recv_sem=e_recv.at[0],
            device_id={"dp": other}, device_id_type=MESH,
        )

    final(d).start()

    for copy in shift:
        copy.wait_send()

    def settle(j):
        spread(j).wait_send()
        forward(j).wait_send()
        deliver(j).wait_send()

    each(n - 1, lambda i: settle(rising(i + 1)))
    each(n, lambda j: swap(j).wait_send())
    final(other).wait_recv()
    dk_ref[0] = fin[0]
    dv_ref[0] = fin[1]
    final(d).wait_send()


def writer(*refs):
    count = len(refs) // 2
    sem = refs[-1]
    copies = [
        pltpu.make_async_copy(refs[i], refs[count + i], sem.at[i]) for i in range(count)
    ]
    for copy in copies:
        copy.start()
    for copy in copies:
        copy.wait()


def body(n_pp, n, n_dp, queries, keys, values, grad_out, span_order):
    tok, dh = keys.shape[1], keys.shape[2]
    heads = queries.shape[2] // dh
    width = heads * tok
    f32, bf16 = jnp.float32, jnp.bfloat16
    scratch = [
        ((2, n, tok, dh), bf16),
        ((2, width, dh), bf16),
        ((n, tok, width), f32),
        ((n, tok, width), f32),
        ((3, n, 1, width), f32),
        ((2, n * tok, width), bf16),
        ((n, tok, dh), bf16),
        ((n, tok, dh), bf16),
        ((n, tok, dh), bf16),
        ((n, tok, dh), bf16),
        ((tok, dh), f32),
        ((2, tok, dh), bf16),
    ]
    held = sum(math.prod(shape) * jnp.dtype(kind).itemsize for shape, kind in scratch)
    dma = pltpu.SemaphoreType.DMA
    sems = [1, heads, 2, heads, heads, n, n, n, n, n, n, n, n, 1, 1]
    pairs = heads * tok * n * tok
    results = pl.pallas_call(
        functools.partial(kernel, n_pp, n, n_dp, heads),
        out_shape=(
            pltpu.VMEM(queries.shape, bf16),
            pltpu.VMEM(queries.shape, bf16),
            pltpu.VMEM(keys.shape, bf16),
            pltpu.VMEM(values.shape, bf16),
        ),
        in_specs=[pl.BlockSpec(memory_space=pltpu.HBM)] * 5,
        out_specs=[pl.BlockSpec(memory_space=pltpu.VMEM)] * 4,
        scratch_shapes=[pltpu.VMEM(shape, kind) for shape, kind in scratch]
        + [pltpu.SMEM(span_order.shape, jnp.int32)]
        + [dma((count,)) for count in sems],
        compiler_params=pltpu.CompilerParams(
            collective_id=0,
            has_side_effects=True,
            vmem_limit_bytes=60 << 20,
        ),
        cost_estimate=pl.CostEstimate(
            flops=12 * pairs * dh, bytes_accessed=8 * tok * heads * dh, transcendentals=pairs
        ),
        name="attention",
    )(span_order, queries, keys, values, grad_out)
    return pl.pallas_call(
        writer,
        out_shape=[jax.ShapeDtypeStruct(r.shape, r.dtype) for r in results],
        in_specs=[pl.BlockSpec(memory_space=pl.ANY)] * 4,
        out_specs=[pl.BlockSpec(memory_space=pltpu.HBM)] * 4,
        scratch_shapes=[dma((4,))],
        compiler_params=pltpu.CompilerParams(vmem_limit_bytes=4 << 20),
        name="writer",
    )(*results)


def solution(mesh):
    in_specs = (
        P("pp", "cp", "dp"),
        P("pp", "cp", None),
        P("pp", "cp", None),
        P("pp", "cp", "dp"),
        P(),
    )
    out_specs = (P("pp", "cp", "dp"), P("pp", "cp", "dp"), P("pp", "cp", None), P("pp", "cp", None))
    sizes = [mesh.shape[axis] for axis in ("pp", "cp", "dp")]
    return jax.shard_map(
        functools.partial(body, *sizes),
        mesh=mesh, in_specs=in_specs, out_specs=out_specs, check_vma=False,
    )
```

```python
import functools
import math

import jax
import jax.numpy as jnp
from jax import lax
from jax.experimental import pallas as pl
from jax.experimental.pallas import tpu as pltpu
from jax.sharding import PartitionSpec as P

MESH = pl.DeviceIdType.MESH
NEG = -1e30


def each(count, fn):
    if count <= 8:
        for i in range(count):
            fn(i)
    else:

        def step(i, carry):
            fn(i)
            return carry

        lax.fori_loop(0, count, step, 0)


def kernel(
    n_pp, n, n_dp, heads, span_hbm, q_ref, k_ref, v_ref, g_ref,
    o_ref, dq_ref, dk_ref, dv_ref,
    kv, qg, wts, dprob, stat, pair, xsend, xrecv, rsend, rrecv, own, fin, span_ref,
    span_sem, q_sem, kv_sem, g_send, g_recv, s_send, s_recv, f_send, f_recv,
    x_send, x_recv, r_send, r_recv, e_send, e_recv,
):
    tok, dh = kv.shape[2], kv.shape[3]
    half = tok // 2
    scale = 1.0 / math.sqrt(dh)
    f32, bf16 = jnp.float32, jnp.bfloat16
    s = lax.axis_index("pp")
    c = lax.axis_index("cp")
    d = lax.axis_index("dp")
    other = 1 - d
    before = lax.rem(s + n_pp - 1, n_pp)
    after = lax.rem(s + 1, n_pp)

    def rising(i):
        return i - 1 + (i - 1 - c + n) // n

    def falling(i):
        return rising(n - i)

    def nearing(i):
        wrapped = (c + i) // n
        return (1 - wrapped) * (c + i) + wrapped * (n - 1 - i)

    barrier = pltpu.get_barrier_semaphore()
    each(
        n - 1,
        lambda i: pl.semaphore_signal(
            barrier, inc=1, device_id={"cp": rising(i + 1)}, device_id_type=MESH
        ),
    )
    pl.semaphore_signal(barrier, inc=1, device_id={"pp": after}, device_id_type=MESH)
    pl.semaphore_signal(barrier, inc=1, device_id={"dp": other}, device_id_type=MESH)

    load_k = pltpu.make_async_copy(k_ref.at[0], kv.at[0, c], kv_sem.at[0])
    load_v = pltpu.make_async_copy(v_ref.at[0], kv.at[1, c], kv_sem.at[1])
    load_k.start()
    load_v.start()
    load_q = [
        pltpu.make_async_copy(
            q_ref.at[0, :, pl.ds(h * dh, dh)], qg.at[0, pl.ds(h * tok, tok), :], q_sem.at[h]
        )
        for h in range(heads)
    ]
    for copy in load_q:
        copy.start()
    load_span = pltpu.make_async_copy(span_hbm, span_ref, span_sem.at[0])
    load_span.start()
    load_k.wait()
    load_v.wait()

    pl.semaphore_wait(barrier, n + 1)

    def spread(j):
        return pltpu.make_async_remote_copy(
            src_ref=kv.at[d, c], dst_ref=kv.at[d, c],
            send_sem=s_send.at[j], recv_sem=s_recv.at[c],
            device_id={"cp": j}, device_id_type=MESH,
        )

    def arrive(j):
        return pltpu.make_async_remote_copy(
            src_ref=kv.at[d, j], dst_ref=kv.at[d, j],
            send_sem=s_send.at[j], recv_sem=s_recv.at[j],
            device_id={"cp": j}, device_id_type=MESH,
        )

    def forward(j):
        return pltpu.make_async_remote_copy(
            src_ref=kv.at[d, j], dst_ref=kv.at[d, j],
            send_sem=f_send.at[j], recv_sem=f_recv.at[j],
            device_id={"dp": other}, device_id_type=MESH,
        )

    def forwarded(j):
        return pltpu.make_async_remote_copy(
            src_ref=kv.at[other, j], dst_ref=kv.at[other, j],
            send_sem=f_send.at[j], recv_sem=f_recv.at[j],
            device_id={"dp": other}, device_id_type=MESH,
        )

    each(n - 1, lambda i: spread(falling(i + 1)).start())
    shift = [
        pltpu.make_async_remote_copy(
            src_ref=g_ref.at[0, :, pl.ds(h * dh, dh)],
            dst_ref=qg.at[1, pl.ds(h * tok, tok), :],
            send_sem=g_send.at[h], recv_sem=g_recv.at[h],
            device_id={"pp": before}, device_id_type=MESH,
        )
        for h in range(heads)
    ]
    for copy in shift:
        copy.start()

    load_span.wait()
    row = lax.broadcasted_iota(jnp.int32, (tok, tok), 0)
    col = lax.broadcasted_iota(jnp.int32, (tok, tok), 1)
    within_row = lax.rem(row, half)
    query_pos = jnp.where(col < half, span_ref[2 * c], span_ref[2 * c + 1]) * half + lax.rem(col, half)
    nt = (((1,), (1,)), ((), ()))

    def block(j):
        return pl.ds(pl.multiple_of(j * tok, tok), tok)

    def scores_of(j):
        key_pos = jnp.where(row < half, span_ref[2 * j], span_ref[2 * j + 1]) * half + within_row
        visible = key_pos <= query_pos
        raw = lax.dot_general(kv[0, j], qg[0], nt, preferred_element_type=f32) * scale
        for h in range(heads):
            cols = slice(h * tok, (h + 1) * tok)
            part = jnp.where(visible, raw[:, cols], NEG)
            peak = jnp.max(part, axis=0, keepdims=True)
            weight = jnp.where(visible, jnp.exp(part - peak), 0.0)
            wts[j, :, cols] = weight
            stat[0, j, :, cols] = peak
            stat[1, j, :, cols] = jnp.sum(weight, axis=0, keepdims=True)

    def grads_of(j):
        grad = lax.dot_general(kv[1, j], qg[1], nt, preferred_element_type=f32)
        dprob[j] = grad
        stat[2, j] = jnp.sum(grad * wts[j], axis=0, keepdims=True)

    for copy in load_q:
        copy.wait()
    scores_of(c)

    def take(i):
        arrive(nearing(i)).wait_recv()
        forward(nearing(i)).start()

    def use(i):
        forwarded(nearing(i)).wait_recv()
        scores_of(nearing(i))

    def take_and_use(i):
        take(i + 2)
        use(i + 1)

    each(n - 1, lambda i: take(i + 1))
    each(n - 2, lambda i: use(i + 1))
    for copy in shift:
        copy.wait_recv()
    grads_of(c)
    each(n - 2, lambda i: grads_of(nearing(i + 1)))
    use(n - 1)
    grads_of(nearing(n - 1))

    peaks = stat[0]
    peak = jnp.max(peaks, axis=0, keepdims=True)
    factor = jnp.exp(peaks - peak)
    total = jnp.sum(factor * stat[1], axis=0, keepdims=True)
    factor = factor / total
    dots = jnp.sum(factor * stat[2], axis=0)
    stat[0] = factor

    share_scale = jnp.where(d == 0, scale, 1.0).astype(f32)
    other_scale = jnp.where(d == 0, 1.0, scale).astype(f32)

    def swap(j):
        return pltpu.make_async_remote_copy(
            src_ref=xsend.at[j], dst_ref=xrecv.at[j],
            send_sem=x_send.at[j], recv_sem=x_recv.at[j],
            device_id={"dp": other}, device_id_type=MESH,
        )

    def deliver(j):
        return pltpu.make_async_remote_copy(
            src_ref=rsend.at[j], dst_ref=rrecv.at[c],
            send_sem=r_send.at[j], recv_sem=r_recv.at[c],
            device_id={"cp": j}, device_id_type=MESH,
        )

    def delivered(j):
        return pltpu.make_async_remote_copy(
            src_ref=rsend.at[j], dst_ref=rrecv.at[j],
            send_sem=r_send.at[j], recv_sem=r_recv.at[j],
            device_id={"cp": j}, device_id_type=MESH,
        )

    def give(j):
        prob = wts[j] * stat[0, j]
        pair[1, block(j), :] = prob.astype(bf16)
        pair[0, block(j), :] = (prob * (dprob[j] - dots)).astype(bf16)
        part = jnp.dot(pair[other, block(j), :], qg[other], preferred_element_type=f32)
        xsend[j] = (part * other_scale).astype(bf16)
        swap(j).start()


    def keep(j):
        part = jnp.dot(pair[d, block(j), :], qg[d], preferred_element_type=f32) * share_scale
        swap(j).wait_recv()
        return part + xrecv[j].astype(f32)

    def send(j):
        rsend[j] = keep(j).astype(bf16)
        deliver(j).start()

    each(n - 1, lambda i: give(rising(i + 1)))
    send(rising(1))
    give(c)
    each(n - 2, lambda i: send(rising(i + 2)))
    own[...] = keep(c)

    tn = (((0,), (0,)), ((), ()))
    keys_all = kv[0].reshape(n * tok, dh)
    values_all = kv[1].reshape(n * tok, dh)
    out_t = lax.dot_general(values_all, pair[1], tn, preferred_element_type=f32)
    for h in range(heads):
        o_ref[0, :, h * dh:(h + 1) * dh] = out_t[:, h * tok:(h + 1) * tok].T.astype(bf16)
    dq_t = lax.dot_general(keys_all, pair[0], tn, preferred_element_type=f32) * scale
    for h in range(heads):
        dq_ref[0, :, h * dh:(h + 1) * dh] = dq_t[:, h * tok:(h + 1) * tok].T.astype(bf16)

    def gather(j):
        delivered(j).wait_recv()
        own[...] += rrecv[j].astype(f32)

    each(n - 1, lambda i: gather(rising(i + 1)))
    fin[d] = own[...].astype(bf16)

    def final(share):
        return pltpu.make_async_remote_copy(
            src_ref=fin.at[share], dst_ref=fin.at[share],
            send_sem=e_send.at[0], recv_sem=e_recv.at[0],
            device_id={"dp": other}, device_id_type=MESH,
        )

    final(d).start()

    for copy in shift:
        copy.wait_send()

    def settle(j):
        spread(j).wait_send()
        forward(j).wait_send()
        deliver(j).wait_send()

    each(n - 1, lambda i: settle(rising(i + 1)))
    each(n, lambda j: swap(j).wait_send())
    final(other).wait_recv()
    dk_ref[0] = fin[0]
    dv_ref[0] = fin[1]
    final(d).wait_send()


def writer(*refs):
    count = len(refs) // 2
    sem = refs[-1]
    copies = [
        pltpu.make_async_copy(refs[i], refs[count + i], sem.at[i]) for i in range(count)
    ]
    for copy in copies:
        copy.start()
    for copy in copies:
        copy.wait()


def body(n_pp, n, n_dp, queries, keys, values, grad_out, span_order):
    tok, dh = keys.shape[1], keys.shape[2]
    heads = queries.shape[2] // dh
    width = heads * tok
    f32, bf16 = jnp.float32, jnp.bfloat16
    scratch = [
        ((2, n, tok, dh), bf16),
        ((2, width, dh), bf16),
        ((n, tok, width), f32),
        ((n, tok, width), f32),
        ((3, n, 1, width), f32),
        ((2, n * tok, width), bf16),
        ((n, tok, dh), bf16),
        ((n, tok, dh), bf16),
        ((n, tok, dh), bf16),
        ((n, tok, dh), bf16),
        ((tok, dh), f32),
        ((2, tok, dh), bf16),
    ]
    held = sum(math.prod(shape) * jnp.dtype(kind).itemsize for shape, kind in scratch)
    dma = pltpu.SemaphoreType.DMA
    sems = [1, heads, 2, heads, heads, n, n, n, n, n, n, n, n, 1, 1]
    pairs = heads * tok * n * tok
    results = pl.pallas_call(
        functools.partial(kernel, n_pp, n, n_dp, heads),
        out_shape=(
            pltpu.VMEM(queries.shape, bf16),
            pltpu.VMEM(queries.shape, bf16),
            pltpu.VMEM(keys.shape, bf16),
            pltpu.VMEM(values.shape, bf16),
        ),
        in_specs=[pl.BlockSpec(memory_space=pltpu.HBM)] * 5,
        out_specs=[pl.BlockSpec(memory_space=pltpu.VMEM)] * 4,
        scratch_shapes=[pltpu.VMEM(shape, kind) for shape, kind in scratch]
        + [pltpu.SMEM(span_order.shape, jnp.int32)]
        + [dma((count,)) for count in sems],
        compiler_params=pltpu.CompilerParams(
            collective_id=0,
            has_side_effects=True,
            vmem_limit_bytes=60 << 20,
        ),
        cost_estimate=pl.CostEstimate(
            flops=12 * pairs * dh, bytes_accessed=8 * tok * heads * dh, transcendentals=pairs
        ),
        name="attention",
    )(span_order, queries, keys, values, grad_out)
    return pl.pallas_call(
        writer,
        out_shape=[jax.ShapeDtypeStruct(r.shape, r.dtype) for r in results],
        in_specs=[pl.BlockSpec(memory_space=pl.ANY)] * 4,
        out_specs=[pl.BlockSpec(memory_space=pltpu.HBM)] * 4,
        scratch_shapes=[dma((4,))],
        compiler_params=pltpu.CompilerParams(vmem_limit_bytes=4 << 20),
        name="writer",
    )(*results)


def solution(mesh):
    in_specs = (
        P("pp", "cp", "dp"),
        P("pp", "cp", None),
        P("pp", "cp", None),
        P("pp", "cp", "dp"),
        P(),
    )
    out_specs = (P("pp", "cp", "dp"), P("pp", "cp", "dp"), P("pp", "cp", None), P("pp", "cp", None))
    sizes = [mesh.shape[axis] for axis in ("pp", "cp", "dp")]
    return jax.shard_map(
        functools.partial(body, *sizes),
        mesh=mesh, in_specs=in_specs, out_specs=out_specs, check_vma=False,
    )
```
